32 devices in a mesh: prow: 8 (over z, x), pcol: 4 (over y, core).
Axes of the slice: x: 2, y: 2, z: 4, core: 2. Of those that a mesh axis runs over, the one named last changes fastest.
Arguments:
- separator_inverse: float32 [12288, 12288], P('prow', 'pcol'), may hold values from -6 to 6
- panel: float32 [12288, 2048], P('pcol', 'prow'), may hold values from -0.0546875 to 0.0546875
- block_rows: int32 [16], replicated, may hold values 0 or 1
- pivot_inverse: float32 [2048, 2048], P('prow', 'pcol'), may hold values from -4 to 4
Outputs:
- off_diagonal: float32 [12288, 2048], P('prow', 'pcol')
- child_inverse: float32 [2048, 2048], P('prow', 'pcol')
The draws below stay inside these ranges and needn't reach their ends.
All inputs are finite; a program needn't handle non-finite values.
Results may differ from the reference program's by a relative error of at most 0.000088.
Values sent between devices are 32-bit elements; how exact they have to be, the bound alone decides.
A program may use at most 128 MiB of HBM per device.

```python
import jax
import jax.numpy as jnp
from jax import lax

BS = 768
NB = 16
CW = 2048
NSEP = 12288


def touch_ends(drawn, key, least, high):
    place = [jax.random.randint(jax.random.fold_in(key, axis), (), 0, length) for axis, length in enumerate(drawn.shape)]
    main_axis = drawn.shape.index(max(drawn.shape))
    neighbour = place[:main_axis] + [(place[main_axis] + 1) % drawn.shape[main_axis]] + place[main_axis + 1:]
    return drawn.at[tuple(place)].set(least).at[tuple(neighbour)].set(high)


def block_levels(rng, extent, split, smallest, top_value):
    level, own = 1.0, jax.random.fold_in(rng, 6)
    for dim, parts in split:
        steps = jnp.exp(jax.random.uniform(jax.random.fold_in(own, dim), (parts,), jnp.float32, smallest / len(split), top_value / len(split)))
        level = level * jnp.repeat(steps, extent[dim] // parts).reshape([-1 if axis == dim else 1 for axis in range(len(extent))])
    return level


def gaussian(key, extent, deviation, most, shards=(), dtype=jnp.bfloat16):
    array = jax.random.normal(key, extent, jnp.float32) * deviation
    if len(shards) > 0:
        array = block_levels(key, extent, shards, -0.22, 0.18) * array
    return jnp.clip(array, min=-most, max=most).astype(dtype)


def setup_inputs(seed: int = 0) -> dict:
    streams_of = jax.random.split(jax.random.key(seed), 5)
    return {
        "separator_inverse": gaussian(streams_of[0], (NSEP, NSEP), 1.0, 6.0, ((0, 8), (1, 4)), jnp.float32),
        "panel": gaussian(streams_of[1], (NSEP, CW), NSEP ** -0.5, 0.0546875, ((0, 4), (1, 8)), jnp.float32),
        "block_rows": touch_ends((jax.random.randint(streams_of[2], (NB,), 0, 4) < 3).astype(jnp.int32), jax.random.fold_in(streams_of[2], 1), 0, 1),
        "pivot_inverse": gaussian(streams_of[3], (CW, CW), 0.5, 4.0, ((0, 8), (1, 4)), jnp.float32),
    }


def reference(separator_inverse, panel, block_rows, pivot_inverse):
    keep = jnp.repeat(block_rows.astype(jnp.float32), BS)
    masked = panel * keep[:, None]
    column_sums = jnp.dot(separator_inverse, masked, precision=lax.Precision.HIGHEST, preferred_element_type=jnp.float32)
    off_diagonal = -(column_sums * keep[:, None])
    gram = jnp.dot(masked.T, off_diagonal, precision=lax.Precision.HIGHEST, preferred_element_type=jnp.float32)
    child_inverse = pivot_inverse - gram
    return off_diagonal, child_inverse
```

```python
import functools

import jax
import jax.numpy as jnp
from jax import lax
from jax.experimental import pallas as pl
from jax.experimental.pallas import tpu as pltpu
from jax.sharding import PartitionSpec as P

BS = 768
PIECES = 2
STRIP = 64
TILE_ROWS = 512
TILE_DEPTH = 1024
VMEM_BYTES = 62 * 1024 * 1024
MESH = pl.DeviceIdType.MESH


def product(left, right, dims):
    return lax.dot_general(
        left,
        right,
        (dims, ((), ())),
        precision=lax.Precision.HIGH,
        preferred_element_type=jnp.float32,
    )


def spread(value, root, row_index, col_index, rows, cols):
    held = jnp.where(col_index == root, value, 0)
    done = 0
    bit = cols // 2
    while bit:
        pairs = []
        for r in range(rows):
            start = r * cols // rows
            for c in range(cols):
                if (c ^ start) & ~done == 0:
                    pairs.append((r * cols + c, r * cols + (c ^ bit)))
        held = held + lax.ppermute(held, ("prow", "pcol"), pairs)
        done |= bit
        bit //= 2
    return held


def local(separator_inverse, panel, block_rows, pivot_inverse):
    local_rows, local_cols = separator_inverse.shape
    rows, cols = lax.axis_size("prow"), lax.axis_size("pcol")
    row_index, col_index = lax.axis_index("prow"), lax.axis_index("pcol")
    row_blocks, col_blocks = local_rows // BS, local_cols // BS
    col_keep = lax.dynamic_slice_in_dim(block_rows, col_index * col_blocks, col_blocks)
    row_keep = lax.dynamic_slice_in_dim(block_rows, row_index * row_blocks, row_blocks)
    col_keep = jnp.repeat(col_keep.astype(jnp.float32), BS)
    row_keep = jnp.repeat(row_keep.astype(jnp.float32), BS)
    masked = panel * col_keep[:, None]
    width = panel.shape[1]
    piece = max(width // PIECES, 128)
    pieces = width // piece
    group = rows // cols
    offset = row_index * local_rows - col_index * local_cols
    root = row_index * cols // rows
    lefts, rights = [], []
    for g in range(pieces):
        whole = lax.all_gather(masked[:, g * piece : (g + 1) * piece], "prow", axis=1, tiled=True)
        source = lax.dynamic_slice_in_dim(whole, offset, local_rows, 0)
        lefts.append(spread(source, root, row_index, col_index, rows, cols))
        part = product(whole, separator_inverse, ((0,), (1,)))
        share = lax.psum_scatter(part, "pcol", scatter_dimension=0, tiled=True)
        rights.append(share * row_keep[None, :])
    kept = jnp.stack([v.reshape(group, piece, local_rows) for v in rights], axis=1)
    kept = kept.reshape(group * width, local_rows)
    left = jnp.stack([v.reshape(local_rows, rows, piece) for v in lefts], axis=2)
    left = left.reshape(local_rows, rows * width)
    gram_part = product(left, kept, ((0,), (1,)))
    gram_share = lax.psum_scatter(gram_part, "prow", scatter_dimension=0, tiled=True)
    return (-kept.T, pivot_inverse + gram_share)


def device_kernel(geometry, sep_ref, panel_ref, colmask_ref, rowmask_ref, off_ref, mr_ref,
                  s_hi, s_lo, m_buf, m_hi, m_lo, p_buf, near, far,
                  load_sem, own_sem, gather_send, gather_recv, p_send, near_recv,
                  far_send, far_recv, root_send, root_recv, root_own, out_sem):
    rows, cols, span = geometry
    local_rows, local_cols = s_hi.shape
    width = m_buf.shape[2]
    r, c = lax.axis_index("prow"), lax.axis_index("pcol")
    z, x = r // 2, lax.rem(r, 2)
    y, core = c // 2, lax.rem(c, 2)
    across = (z * 2 + 1 - x, c)
    above, below = (r + 2, c), (r - 2, c)
    mate = (r, y * 2 + 1 - core)
    other = (r, (1 - y) * 2 + core)
    has_above, has_below = z < span - 1, z > 0
    is_root = c == z
    is_relay = c == lax.rem(z + 2, 4)

    own = pltpu.make_async_copy(panel_ref, m_buf.at[r], own_sem)
    own.start()

    def tile(i):
        return pltpu.make_async_copy(
            sep_ref.at[:, pl.ds(pl.multiple_of(i * width, width), width)],
            p_buf.at[lax.rem(i, 2)], load_sem.at[lax.rem(i, 2)])

    tile(0).start()

    barrier = pltpu.get_barrier_semaphore()
    for peer in (across, mate, other):
        pl.semaphore_signal(barrier, inc=1, device_id=peer, device_id_type=MESH)

    @pl.when(has_above)
    def _():
        pl.semaphore_signal(barrier, inc=1, device_id=above, device_id_type=MESH)

    @pl.when(has_below)
    def _():
        pl.semaphore_signal(barrier, inc=1, device_id=below, device_id_type=MESH)

    pl.semaphore_wait(barrier, 3 + has_above.astype(jnp.int32) + has_below.astype(jnp.int32))

    def place(k):
        partner = jnp.logical_or(jnp.logical_and(k >= 2, lax.rem(k, 2) == 0), k == 7)
        j = jnp.where(partner, jnp.where(k == 7, 3, (k - 2) // 2), (k + 1) // 2)
        inner = jnp.logical_and(z > 0, z < span - 1)
        q = jnp.where(jnp.logical_and(inner, j < 2), 1 - j, j)
        source_z = jnp.where(z < 2, q, span - 1 - q)
        return source_z * 2 + jnp.where(partner, 1 - x, x), source_z, partner

    def gather(slot, way, target):
        return pltpu.make_async_remote_copy(
            src_ref=m_buf.at[slot], dst_ref=m_buf.at[slot],
            send_sem=gather_send.at[way, slot], recv_sem=gather_recv.at[slot],
            device_id=target, device_id_type=MESH)

    def forwards(slot, source_z, partner, act):
        line = jnp.logical_not(partner)

        @pl.when(line)
        def _():
            act(gather(slot, 0, across))

        @pl.when(jnp.logical_and(line, jnp.logical_and(source_z <= z, has_above)))
        def _():
            act(gather(slot, 1, above))

        @pl.when(jnp.logical_and(line, jnp.logical_and(source_z >= z, has_below)))
        def _():
            act(gather(slot, 2, below))

    def to_mate(slot):
        return pltpu.make_async_remote_copy(
            src_ref=m_buf.at[slot, pl.ds(pl.multiple_of(x * local_rows, local_rows), local_rows)],
            dst_ref=mr_ref.at[slot], send_sem=root_send.at[0, slot], recv_sem=root_recv.at[slot],
            device_id=mate, device_id_type=MESH)

    def to_other(slot):
        return pltpu.make_async_remote_copy(
            src_ref=m_buf.at[slot, pl.ds(pl.multiple_of(x * local_rows, local_rows), local_rows)],
            dst_ref=mr_ref.at[slot], send_sem=root_send.at[1, slot], recv_sem=root_recv.at[slot],
            device_id=other, device_id_type=MESH)

    def relay(slot):
        return pltpu.make_async_remote_copy(
            src_ref=mr_ref.at[slot], dst_ref=mr_ref.at[slot],
            send_sem=root_send.at[0, slot], recv_sem=root_recv.at[slot],
            device_id=mate, device_id_type=MESH)

    def keep_own(slot):
        return pltpu.make_async_copy(
            m_buf.at[slot, pl.ds(pl.multiple_of(x * local_rows, local_rows), local_rows)],
            mr_ref.at[slot], root_own.at[slot])

    def partial(slot):
        i = (slot // 4) * 2 + lax.rem(slot, 2)
        return pltpu.make_async_remote_copy(
            src_ref=p_buf.at[0], dst_ref=near.at[i], send_sem=p_send, recv_sem=near_recv.at[i],
            device_id=mate, device_id_type=MESH)

    def chip_sum(slot):
        b = lax.rem(slot, 2)
        return pltpu.make_async_remote_copy(
            src_ref=near.at[(slot // 4) * 2 + b], dst_ref=far.at[b],
            send_sem=far_send.at[b], recv_sem=far_recv.at[b],
            device_id=other, device_id_type=MESH)

    def core_of(slot):
        return lax.rem(slot // 2, 2)

    own.wait()
    forwards(r, z, jnp.bool_(False), lambda copy: copy.start())

    tiles = local_cols // width

    def split(i, carry):
        @pl.when(i + 1 < tiles)
        def _():
            tile(i + 1).start()

        tile(i).wait()
        columns = pl.ds(pl.multiple_of(i * width, width), width)

        def strip(t, inner):
            part = pl.ds(pl.multiple_of(t * STRIP, STRIP), STRIP)
            value = p_buf[lax.rem(i, 2), part, :] * colmask_ref[:, columns] * rowmask_ref[part, :]
            high = value.astype(jnp.bfloat16)
            s_hi[part, columns] = high
            s_lo[part, columns] = (value - high.astype(jnp.float32)).astype(jnp.bfloat16)
            return inner

        return lax.fori_loop(0, local_rows // STRIP, strip, carry)

    lax.fori_loop(0, tiles, split, 0)

    def relay_at(k):
        slot, _, _ = place(k)

        @pl.when(is_relay)
        def _():
            relay(slot).wait_recv()
            relay(slot).start()

    def step(k, carry):
        slot, source_z, partner = place(k)

        @pl.when(k > 0)
        def _():
            gather(slot, 0, across).wait_recv()
            forwards(slot, source_z, partner, lambda copy: copy.start())

        @pl.when(is_root)
        def _():
            to_other(slot).start()
            to_mate(slot).start()
            keep_own(slot).start()

        @pl.when(k > 0)
        def _():
            before, _, _ = place(k - 1)

            @pl.when(core_of(before) != core)
            def _():
                partial(before).wait_send()

        def cut(t, inner):
            part = pl.ds(pl.multiple_of(t * STRIP, STRIP), STRIP)
            value = m_buf[slot, part, :]
            high = value.astype(jnp.bfloat16)
            m_hi[part, :] = high
            m_lo[part, :] = (value - high.astype(jnp.float32)).astype(jnp.bfloat16)
            return inner

        lax.fori_loop(0, local_cols // STRIP, cut, 0)

        def multiply(t, inner):
            part = pl.ds(pl.multiple_of(t * TILE_ROWS, TILE_ROWS), TILE_ROWS)
            total = None
            for d in range(local_cols // TILE_DEPTH):
                depth = pl.ds(d * TILE_DEPTH, TILE_DEPTH)
                a, b = s_hi[part, depth], s_lo[part, depth]
                u, v = m_hi[depth, :], m_lo[depth, :]
                term = (jnp.dot(a, u, preferred_element_type=jnp.float32)
                        + jnp.dot(a, v, preferred_element_type=jnp.float32)
                        + jnp.dot(b, u, preferred_element_type=jnp.float32))
                total = term if total is None else total + term
            p_buf[0, part, :] = total
            return inner

        lax.fori_loop(0, local_rows // TILE_ROWS, multiply, 0)

        @pl.when(core_of(slot) != core)
        def _():
            partial(slot).start()

        @pl.when(k > 0)
        def _():
            relay_at(k - 1)

        @pl.when(core_of(slot) == core)
        def _():
            partial(slot).wait_recv()
            i = (slot // 4) * 2 + lax.rem(slot, 2)

            def add(t, inner):
                part = pl.ds(pl.multiple_of(t * STRIP, STRIP), STRIP)
                near[i, part, :] += p_buf[0, part, :]
                return inner

            lax.fori_loop(0, local_rows // STRIP, add, 0)

            @pl.when(slot // 4 != y)
            def _():
                chip_sum(slot).start()

        return carry

    lax.fori_loop(0, rows, step, 0)

    last, _, _ = place(rows - 1)

    @pl.when(core_of(last) != core)
    def _():
        partial(last).wait_send()

    relay_at(rows - 1)

    def finish(b):
        return pltpu.make_async_copy(
            near.at[y * 2 + b], off_ref.at[:, pl.ds(b * width, width)], out_sem.at[b])

    for b in range(2):
        mine = c * 2 + b
        chip_sum(mine).wait_recv()

        def total(t, inner):
            part = pl.ds(pl.multiple_of(t * STRIP, STRIP), STRIP)
            near[y * 2 + b, part, :] += far[b, part, :]
            return inner

        lax.fori_loop(0, local_rows // STRIP, total, 0)
        finish(b).start()

    def drain(k, carry):
        slot, source_z, partner = place(k)
        forwards(slot, source_z, partner, lambda copy: copy.wait_send())

        @pl.when(is_root)
        def _():
            to_other(slot).wait_send()
            to_mate(slot).wait_send()
            keep_own(slot).wait()

        @pl.when(is_relay)
        def _():
            relay(slot).wait_send()

        @pl.when(jnp.logical_not(jnp.logical_or(is_root, is_relay)))
        def _():
            relay(slot).wait_recv()

        return carry

    lax.fori_loop(0, rows, drain, 0)
    for b in range(2):
        chip_sum((1 - y) * 4 + core * 2 + b).wait_send()
        finish(b).wait()


def fused(separator_inverse, panel, block_rows, pivot_inverse):
    local_rows, local_cols = separator_inverse.shape
    width = panel.shape[1]
    rows, cols = lax.axis_size("prow"), lax.axis_size("pcol")
    row_index, col_index = lax.axis_index("prow"), lax.axis_index("pcol")
    row_blocks, col_blocks = local_rows // BS, local_cols // BS
    col_keep = lax.dynamic_slice_in_dim(block_rows, col_index * col_blocks, col_blocks)
    row_keep = lax.dynamic_slice_in_dim(block_rows, row_index * row_blocks, row_blocks)
    col_mask = jnp.repeat(col_keep.astype(jnp.float32), BS)[None, :]
    row_mask = -jnp.repeat(row_keep.astype(jnp.float32), BS)[:, None]
    dma, f32, bf16 = pltpu.SemaphoreType.DMA, jnp.float32, jnp.bfloat16
    flops = 6 * local_rows * local_cols * rows * width
    off, source = pl.pallas_call(
        functools.partial(device_kernel, (rows, cols, rows // 2)),
        out_shape=(jax.ShapeDtypeStruct((local_rows, 2 * width), f32),
                   jax.ShapeDtypeStruct((rows, local_rows, width), f32)),
        in_specs=[pl.BlockSpec(memory_space=pl.ANY), pl.BlockSpec(memory_space=pl.ANY),
                  pl.BlockSpec(memory_space=pltpu.VMEM), pl.BlockSpec(memory_space=pltpu.VMEM)],
        out_specs=(pl.BlockSpec(memory_space=pl.ANY), pl.BlockSpec(memory_space=pl.ANY)),
        scratch_shapes=[
            pltpu.VMEM((local_rows, local_cols), bf16),
            pltpu.VMEM((local_rows, local_cols), bf16),
            pltpu.VMEM((rows, local_cols, width), f32),
            pltpu.VMEM((local_cols, width), bf16),
            pltpu.VMEM((local_cols, width), bf16),
            pltpu.VMEM((2, local_rows, width), f32),
            pltpu.VMEM((4, local_rows, width), f32),
            pltpu.VMEM((2, local_rows, width), f32),
            dma((2,)), dma, dma((3, rows)), dma((rows,)), dma, dma((4,)),
            dma((2,)), dma((2,)), dma((2, rows)), dma((rows,)), dma((rows,)), dma((2,)),
        ],
        compiler_params=pltpu.CompilerParams(
            collective_id=0, has_side_effects=True, vmem_limit_bytes=VMEM_BYTES),
        cost_estimate=pl.CostEstimate(
            flops=flops, bytes_accessed=4 * local_rows * local_cols, transcendentals=0),
    )(separator_inverse, panel, col_mask, row_mask)
    gram_part = product(source, off, ((1,), (0,))).reshape(rows * width, 2 * width)
    gram_share = lax.psum_scatter(gram_part, "prow", scatter_dimension=0, tiled=True)
    return (off, pivot_inverse - gram_share)


def solution(mesh):
    in_specs = (P("prow", "pcol"), P("pcol", "prow"), P(), P("prow", "pcol"))
    out_specs = (P("prow", "pcol"), P("prow", "pcol"))
    body = fused if (mesh.shape["prow"], mesh.shape["pcol"]) == (8, 4) else local
    return jax.shard_map(body, mesh=mesh, in_specs=in_specs, out_specs=out_specs, check_vma=False)
```

```python
import functools

import jax
import jax.numpy as jnp
from jax import lax
from jax.experimental import pallas as pl
from jax.experimental.pallas import tpu as pltpu
from jax.sharding import PartitionSpec as P

BS = 768
PIECES = 2
STRIP = 64
TILE_ROWS = 512
TILE_DEPTH = 1024
EARLY = 2560
VMEM_BYTES = 62 * 1024 * 1024
MESH = pl.DeviceIdType.MESH


def product(left, right, dims):
    return lax.dot_general(
        left,
        right,
        (dims, ((), ())),
        precision=lax.Precision.HIGH,
        preferred_element_type=jnp.float32,
    )


def spread(value, root, row_index, col_index, rows, cols):
    held = jnp.where(col_index == root, value, 0)
    done = 0
    bit = cols // 2
    while bit:
        pairs = []
        for r in range(rows):
            start = r * cols // rows
            for c in range(cols):
                if (c ^ start) & ~done == 0:
                    pairs.append((r * cols + c, r * cols + (c ^ bit)))
        held = held + lax.ppermute(held, ("prow", "pcol"), pairs)
        done |= bit
        bit //= 2
    return held


def local(separator_inverse, panel, block_rows, pivot_inverse):
    local_rows, local_cols = separator_inverse.shape
    rows, cols = lax.axis_size("prow"), lax.axis_size("pcol")
    row_index, col_index = lax.axis_index("prow"), lax.axis_index("pcol")
    row_blocks, col_blocks = local_rows // BS, local_cols // BS
    col_keep = lax.dynamic_slice_in_dim(block_rows, col_index * col_blocks, col_blocks)
    row_keep = lax.dynamic_slice_in_dim(block_rows, row_index * row_blocks, row_blocks)
    col_keep = jnp.repeat(col_keep.astype(jnp.float32), BS)
    row_keep = jnp.repeat(row_keep.astype(jnp.float32), BS)
    masked = panel * col_keep[:, None]
    width = panel.shape[1]
    piece = max(width // PIECES, 128)
    pieces = width // piece
    group = rows // cols
    offset = row_index * local_rows - col_index * local_cols
    root = row_index * cols // rows
    lefts, rights = [], []
    for g in range(pieces):
        whole = lax.all_gather(masked[:, g * piece : (g + 1) * piece], "prow", axis=1, tiled=True)
        source = lax.dynamic_slice_in_dim(whole, offset, local_rows, 0)
        lefts.append(spread(source, root, row_index, col_index, rows, cols))
        part = product(whole, separator_inverse, ((0,), (1,)))
        share = lax.psum_scatter(part, "pcol", scatter_dimension=0, tiled=True)
        rights.append(share * row_keep[None, :])
    kept = jnp.stack([v.reshape(group, piece, local_rows) for v in rights], axis=1)
    kept = kept.reshape(group * width, local_rows)
    left = jnp.stack([v.reshape(local_rows, rows, piece) for v in lefts], axis=2)
    left = left.reshape(local_rows, rows * width)
    gram_part = product(left, kept, ((0,), (1,)))
    gram_share = lax.psum_scatter(gram_part, "prow", scatter_dimension=0, tiled=True)
    return (-kept.T, pivot_inverse + gram_share)


def device_kernel(geometry, sep_ref, panel_ref, colmask_ref, rowmask_ref, pivot_ref,
                  off_ref, child_ref, mr_ref, gram_z,
                  s_hi, s_lo, m_buf, m_hi, m_lo, p_buf, near, far, gram_x,
                  load_sem, own_sem, gather_send, gather_recv, late_send, late_recv,
                  p_send, near_recv, far_send, far_recv, root_send, root_recv, root_own, out_sem,
                  rows_sem, x_send, x_recv, z_send, z_recv, pivot_sem, child_sem, stage_sem):
    rows, cols, span = geometry
    local_rows, local_cols = s_hi.shape
    width = m_buf.shape[2]
    r, c = lax.axis_index("prow"), lax.axis_index("pcol")
    z, x = r // 2, lax.rem(r, 2)
    y, core = c // 2, lax.rem(c, 2)
    across = (z * 2 + 1 - x, c)
    above, below = (r + 2, c), (r - 2, c)
    mate = (r, y * 2 + 1 - core)
    other = (r, (1 - y) * 2 + core)
    has_above, has_below = z < span - 1, z > 0
    is_root = c == z
    is_relay = c == lax.rem(z + 2, 4)

    own = pltpu.make_async_copy(panel_ref, m_buf.at[r], own_sem)
    own.start()

    half = local_rows // 2

    def tile(i):
        part = pl.ds(pl.multiple_of(lax.rem(i, 2) * half, half), half)
        return pltpu.make_async_copy(
            sep_ref.at[part, pl.ds(pl.multiple_of((i // 2) * width, width), width)],
            p_buf.at[part], load_sem.at[lax.rem(i, 2)])

    tile(0).start()

    barrier = pltpu.get_barrier_semaphore()
    for peer in (across, mate, other):
        pl.semaphore_signal(barrier, inc=1, device_id=peer, device_id_type=MESH)

    @pl.when(has_above)
    def _():
        pl.semaphore_signal(barrier, inc=1, device_id=above, device_id_type=MESH)

    @pl.when(has_below)
    def _():
        pl.semaphore_signal(barrier, inc=1, device_id=below, device_id_type=MESH)

    pl.semaphore_wait(barrier, 3 + has_above.astype(jnp.int32) + has_below.astype(jnp.int32))

    def line(j):
        inner = jnp.logical_and(z > 0, z < span - 1)
        q = jnp.where(jnp.logical_and(inner, j < 2), 1 - j, j)
        return jnp.where(z < 2, q, span - 1 - q)

    def place(k):
        partner = jnp.logical_or(jnp.logical_and(k >= 2, lax.rem(k, 2) == 0), k == 7)
        j = jnp.where(partner, jnp.where(k == 7, 3, (k - 2) // 2), (k + 1) // 2)
        source_z = line(j)
        return source_z * 2 + jnp.where(partner, 1 - x, x), source_z, partner

    def gather(slot, way, target):
        part = pl.ds(0, EARLY)
        return pltpu.make_async_remote_copy(
            src_ref=m_buf.at[slot, part], dst_ref=m_buf.at[slot, part],
            send_sem=gather_send.at[way, slot], recv_sem=gather_recv.at[slot],
            device_id=target, device_id_type=MESH)

    def gather_late(slot, way, target):
        part = pl.ds(EARLY, local_cols - EARLY)
        return pltpu.make_async_remote_copy(
            src_ref=m_buf.at[slot, part], dst_ref=m_buf.at[slot, part],
            send_sem=late_send.at[way, slot], recv_sem=late_recv.at[slot],
            device_id=target, device_id_type=MESH)

    def goes_up(source_z):
        return jnp.logical_and(source_z <= z, has_above)

    def goes_down(source_z):
        return jnp.logical_and(source_z >= z, has_below)

    def along(copy, slot, source_z, act):
        @pl.when(goes_up(source_z))
        def _():
            act(copy(slot, 1, above))

        @pl.when(goes_down(source_z))
        def _():
            act(copy(slot, 2, below))

    def forwards(slot, source_z, partner, act):
        @pl.when(jnp.logical_not(partner))
        def _():
            @pl.when(source_z == z)
            def _():
                act(gather_late(slot, 0, across))

            along(gather_late, slot, source_z, act)
            along(gather, slot, source_z, act)
            act(gather(slot, 0, across))

    def passes_on(source_z):
        return jnp.logical_or(goes_up(source_z), goes_down(source_z))

    def pass_on(j):
        source_z = line(j)
        slot = source_z * 2 + 1 - x

        @pl.when(passes_on(source_z))
        def _():
            gather_late(slot, 0, across).wait_recv()
            along(gather_late, slot, source_z, lambda copy: copy.start())

    def to_mate(slot):
        return pltpu.make_async_remote_copy(
            src_ref=m_buf.at[slot, pl.ds(pl.multiple_of(x * local_rows, local_rows), local_rows)],
            dst_ref=mr_ref.at[slot], send_sem=root_send.at[0, slot], recv_sem=root_recv.at[slot],
            device_id=mate, device_id_type=MESH)

    def to_other(slot):
        return pltpu.make_async_remote_copy(
            src_ref=m_buf.at[slot, pl.ds(pl.multiple_of(x * local_rows, local_rows), local_rows)],
            dst_ref=mr_ref.at[slot], send_sem=root_send.at[1, slot], recv_sem=root_recv.at[slot],
            device_id=other, device_id_type=MESH)

    def relay(slot):
        return pltpu.make_async_remote_copy(
            src_ref=mr_ref.at[slot], dst_ref=mr_ref.at[slot],
            send_sem=root_send.at[0, slot], recv_sem=root_recv.at[slot],
            device_id=mate, device_id_type=MESH)

    def keep_own(slot):
        return pltpu.make_async_copy(
            m_buf.at[slot, pl.ds(pl.multiple_of(x * local_rows, local_rows), local_rows)],
            mr_ref.at[slot], root_own.at[slot])

    def partial(slot):
        i = (slot // 4) * 2 + lax.rem(slot, 2)
        return pltpu.make_async_remote_copy(
            src_ref=p_buf, dst_ref=near.at[i], send_sem=p_send, recv_sem=near_recv.at[i],
            device_id=mate, device_id_type=MESH)

    def chip_sum(slot):
        b = lax.rem(slot, 2)
        return pltpu.make_async_remote_copy(
            src_ref=near.at[(slot // 4) * 2 + b], dst_ref=far.at[b],
            send_sem=far_send.at[b], recv_sem=far_recv.at[b],
            device_id=other, device_id_type=MESH)

    def core_of(slot):
        return lax.rem(slot // 2, 2)

    own.wait()
    forwards(r, z, jnp.bool_(False), lambda copy: copy.start())

    tiles = 2 * (local_cols // width)

    def split(i, carry):
        @pl.when(i + 1 < tiles)
        def _():
            tile(i + 1).start()

        tile(i).wait()
        columns = pl.ds(pl.multiple_of((i // 2) * width, width), width)

        def strip(t, inner):
            part = pl.ds(pl.multiple_of(lax.rem(i, 2) * half + t * STRIP, STRIP), STRIP)
            value = p_buf[part, :] * colmask_ref[:, columns] * rowmask_ref[(lax.rem(i, 2) * half + t * STRIP) // BS]
            high = value.astype(jnp.bfloat16)
            s_hi[part, columns] = high
            s_lo[part, columns] = (value - high.astype(jnp.float32)).astype(jnp.bfloat16)
            return inner

        return lax.fori_loop(0, half // STRIP, strip, carry)

    lax.fori_loop(0, tiles, split, 0)

    def relay_at(k):
        slot, _, _ = place(k)

        @pl.when(is_relay)
        def _():
            relay(slot).wait_recv()
            relay(slot).start()

    def step(k, carry):
        slot, source_z, partner = place(k)

        @pl.when(k > 0)
        def _():
            gather(slot, 0, across).wait_recv()

            @pl.when(jnp.logical_not(jnp.logical_and(partner, passes_on(source_z))))
            def _():
                gather_late(slot, 0, across).wait_recv()

            forwards(slot, source_z, partner, lambda copy: copy.start())

        for turn, j in ((1, 0), (3, 1), (5, 2), (5, 3)):
            @pl.when(k == turn)
            def _():
                pass_on(j)

        @pl.when(is_root)
        def _():
            to_other(slot).start()
            to_mate(slot).start()
            keep_own(slot).start()

        @pl.when(k > 0)
        def _():
            before, _, _ = place(k - 1)

            @pl.when(core_of(before) != core)
            def _():
                partial(before).wait_send()

        def cut(t, inner):
            part = pl.ds(pl.multiple_of(t * STRIP, STRIP), STRIP)
            value = m_buf[slot, part, :]
            high = value.astype(jnp.bfloat16)
            m_hi[part, :] = high
            m_lo[part, :] = (value - high.astype(jnp.float32)).astype(jnp.bfloat16)
            return inner

        lax.fori_loop(0, local_cols // STRIP, cut, 0)

        def multiply(t, inner):
            part = pl.ds(pl.multiple_of(t * TILE_ROWS, TILE_ROWS), TILE_ROWS)
            total = None
            for d in range(local_cols // TILE_DEPTH):
                depth = pl.ds(d * TILE_DEPTH, TILE_DEPTH)
                a, b = s_hi[part, depth], s_lo[part, depth]
                u, v = m_hi[depth, :], m_lo[depth, :]
                term = (jnp.dot(a, u, preferred_element_type=jnp.float32)
                        + jnp.dot(a, v, preferred_element_type=jnp.float32)
                        + jnp.dot(b, u, preferred_element_type=jnp.float32))
                total = term if total is None else total + term
            p_buf[part, :] = total
            return inner

        lax.fori_loop(0, local_rows // TILE_ROWS, multiply, 0)

        @pl.when(core_of(slot) != core)
        def _():
            partial(slot).start()

        @pl.when(k > 0)
        def _():
            relay_at(k - 1)

        @pl.when(core_of(slot) == core)
        def _():
            partial(slot).wait_recv()
            i = (slot // 4) * 2 + lax.rem(slot, 2)

            def add(t, inner):
                part = pl.ds(pl.multiple_of(t * STRIP, STRIP), STRIP)
                near[i, part, :] += p_buf[part, :]
                return inner

            lax.fori_loop(0, local_rows // STRIP, add, 0)

            @pl.when(slot // 4 != y)
            def _():
                chip_sum(slot).start()

        return carry

    lax.fori_loop(0, rows, step, 0)

    last, _, _ = place(rows - 1)

    @pl.when(core_of(last) != core)
    def _():
        partial(last).wait_send()

    relay_at(rows - 1)

    def own_rows(k):
        slot, _, _ = place(k)
        return pltpu.make_async_copy(
            mr_ref.at[slot], m_buf.at[slot, pl.ds(0, local_rows)], rows_sem.at[slot])

    def drain(k, carry):
        slot, source_z, partner = place(k)
        forwards(slot, source_z, partner, lambda copy: copy.wait_send())

        @pl.when(partner)
        def _():
            along(gather_late, slot, source_z, lambda copy: copy.wait_send())

        @pl.when(is_root)
        def _():
            to_other(slot).wait_send()
            to_mate(slot).wait_send()
            keep_own(slot).wait()

        @pl.when(is_relay)
        def _():
            relay(slot).wait_send()

        @pl.when(jnp.logical_not(jnp.logical_or(is_root, is_relay)))
        def _():
            relay(slot).wait_recv()

        own_rows(k).start()
        return carry

    lax.fori_loop(0, rows, drain, 0)

    def pivot(b):
        return pltpu.make_async_copy(
            pivot_ref.at[:, pl.ds(b * width, width)],
            m_buf.at[0, pl.ds(local_rows + 2 * width + b * width, width)], pivot_sem.at[b])

    def finish(b):
        return pltpu.make_async_copy(
            near.at[y * 2 + b], off_ref.at[:, pl.ds(b * width, width)], out_sem.at[b])

    for b in range(2):
        pivot(b).start()
        mine = c * 2 + b
        chip_sum(mine).wait_recv()

        def total(t, inner):
            part = pl.ds(pl.multiple_of(t * STRIP, STRIP), STRIP)
            value = near[y * 2 + b, part, :] + far[b, part, :]
            near[y * 2 + b, part, :] = value
            high = value.astype(jnp.bfloat16)
            spot = pl.ds(pl.multiple_of(b * local_rows + t * STRIP, STRIP), STRIP)
            m_hi[spot, :] = high
            m_lo[spot, :] = (value - high.astype(jnp.float32)).astype(jnp.bfloat16)
            return inner

        lax.fori_loop(0, local_rows // STRIP, total, 0)
        finish(b).start()

    columns = pl.ds(0, width)

    def gram(slot):
        pltpu.make_async_copy(
            mr_ref.at[slot], m_buf.at[slot, pl.ds(0, local_rows)], rows_sem.at[slot]).wait()

        def cut(t, inner):
            part = pl.ds(pl.multiple_of(t * STRIP, STRIP), STRIP)
            value = m_buf[slot, part, :]
            high = value.astype(jnp.bfloat16)
            s_hi[part, columns] = high
            s_lo[part, columns] = (value - high.astype(jnp.float32)).astype(jnp.bfloat16)
            return inner

        lax.fori_loop(0, local_rows // STRIP, cut, 0)
        for b in range(2):
            sums = None
            for d in range(local_rows // TILE_ROWS):
                part = pl.ds(d * TILE_ROWS, TILE_ROWS)
                spot = pl.ds(b * local_rows + d * TILE_ROWS, TILE_ROWS)
                u, v = s_hi[part, columns], s_lo[part, columns]
                a, e = m_hi[spot, :], m_lo[spot, :]
                term = crossed(u, a) + crossed(u, e) + crossed(v, a)
                sums = term if sums is None else sums + term
            m_buf[slot, pl.ds(local_rows + b * width, width), :] = sums

    block = pl.ds(local_rows, 2 * width)

    def over_x(slot, source_z):
        return pltpu.make_async_remote_copy(
            src_ref=m_buf.at[slot, block], dst_ref=gram_x.at[source_z],
            send_sem=x_send.at[source_z], recv_sem=x_recv.at[source_z],
            device_id=across, device_id_type=MESH)

    def over_z(slot, source_z, spot, target):
        return pltpu.make_async_remote_copy(
            src_ref=m_buf.at[slot, block], dst_ref=gram_z.at[spot],
            send_sem=z_send.at[source_z], recv_sem=z_recv.at[spot],
            device_id=target, device_id_type=MESH)

    def add_to(slot, ref, spot):
        def one(t, inner):
            part = pl.ds(pl.multiple_of(t * STRIP, STRIP), STRIP)
            here = pl.ds(pl.multiple_of(local_rows + t * STRIP, STRIP), STRIP)
            m_buf[slot, here, :] += ref[spot, part, :]
            return inner

        lax.fori_loop(0, 2 * width // STRIP, one, 0)

    stage = local_rows + 4 * width

    def add_staged(slot, spot):
        copy = pltpu.make_async_copy(
            gram_z.at[spot], m_buf.at[slot, pl.ds(stage, 2 * width)], stage_sem)
        copy.start()
        copy.wait()

        def one(t, inner):
            part = pl.ds(pl.multiple_of(stage + t * STRIP, STRIP), STRIP)
            here = pl.ds(pl.multiple_of(local_rows + t * STRIP, STRIP), STRIP)
            m_buf[slot, here, :] += m_buf[slot, part, :]
            return inner

        lax.fori_loop(0, 2 * width // STRIP, one, 0)

    def send_x(i, carry):
        source_z = line(span - 1 - i)
        slot = source_z * 2 + 1 - x
        gram(slot)
        over_x(slot, source_z).start()
        return carry

    lax.fori_loop(0, span, send_x, 0)

    def down_spot(source_z):
        return jnp.where(source_z == z - 1, span, source_z)

    def send_z(i, carry):
        source_z = line(span - 1 - i)
        slot = source_z * 2 + x
        gram(slot)
        over_x(slot, source_z).wait_recv()
        add_to(slot, gram_x, source_z)

        @pl.when(jnp.logical_and(source_z >= z, has_below))
        def _():
            over_z(slot, source_z, source_z, above).wait_recv()
            add_staged(slot, source_z)

        @pl.when(jnp.logical_and(source_z <= z, has_above))
        def _():
            spot = jnp.where(source_z == z, span, source_z)
            over_z(slot, source_z, spot, below).wait_recv()
            add_staged(slot, spot)

        @pl.when(source_z > z)
        def _():
            over_z(slot, source_z, source_z, above).start()

        @pl.when(source_z < z)
        def _():
            over_z(slot, source_z, down_spot(source_z), below).start()

        return carry

    lax.fori_loop(0, span, send_z, 0)

    def child(b):
        return pltpu.make_async_copy(
            p_buf.at[pl.ds(b * width, width)], child_ref.at[:, pl.ds(b * width, width)],
            child_sem.at[b])

    for b in range(2):
        pivot(b).wait()

        def subtract(t, inner):
            part = pl.ds(pl.multiple_of(b * width + t * STRIP, STRIP), STRIP)
            here = pl.ds(pl.multiple_of(local_rows + b * width + t * STRIP, STRIP), STRIP)
            base = pl.ds(pl.multiple_of(local_rows + (2 + b) * width + t * STRIP, STRIP), STRIP)
            p_buf[part, :] = m_buf[0, base, :] - m_buf[r, here, :]
            return inner

        lax.fori_loop(0, width // STRIP, subtract, 0)
        child(b).start()

    def settle(i, carry):
        over_x(i * 2 + 1 - x, i).wait_send()

        @pl.when(i > z)
        def _():
            over_z(i * 2 + x, i, i, above).wait_send()

        @pl.when(i < z)
        def _():
            over_z(i * 2 + x, i, down_spot(i), below).wait_send()

        return carry

    lax.fori_loop(0, span, settle, 0)
    for b in range(2):
        chip_sum((1 - y) * 4 + core * 2 + b).wait_send()
        finish(b).wait()
        child(b).wait()


def crossed(left, right):
    return lax.dot_general(
        left, right, (((0,), (0,)), ((), ())), preferred_element_type=jnp.float32)


def fused(separator_inverse, panel, block_rows, pivot_inverse):
    local_rows, local_cols = separator_inverse.shape
    width = panel.shape[1]
    rows, cols = lax.axis_size("prow"), lax.axis_size("pcol")
    row_index, col_index = lax.axis_index("prow"), lax.axis_index("pcol")
    row_blocks, col_blocks = local_rows // BS, local_cols // BS
    col_keep = lax.dynamic_slice_in_dim(block_rows, col_index * col_blocks, col_blocks)
    row_keep = lax.dynamic_slice_in_dim(block_rows, row_index * row_blocks, row_blocks)
    col_mask = jnp.repeat(col_keep.astype(jnp.float32), BS)[None, :]
    row_mask = -jnp.broadcast_to(
        row_keep.astype(jnp.float32)[:, None, None], (row_blocks, 1, width))
    dma, f32, bf16 = pltpu.SemaphoreType.DMA, jnp.float32, jnp.bfloat16
    flops = 6 * local_rows * local_cols * rows * width
    off, child, _, _ = pl.pallas_call(
        functools.partial(device_kernel, (rows, cols, rows // 2)),
        out_shape=(jax.ShapeDtypeStruct((local_rows, 2 * width), f32),
                   jax.ShapeDtypeStruct((width, 2 * width), f32),
                   jax.ShapeDtypeStruct((rows, local_rows, width), f32),
                   jax.ShapeDtypeStruct((5, 2 * width, width), f32)),
        in_specs=[pl.BlockSpec(memory_space=pl.ANY), pl.BlockSpec(memory_space=pl.ANY),
                  pl.BlockSpec(memory_space=pltpu.VMEM), pl.BlockSpec(memory_space=pltpu.VMEM),
                  pl.BlockSpec(memory_space=pl.ANY)],
        out_specs=(pl.BlockSpec(memory_space=pl.ANY),) * 4,
        scratch_shapes=[
            pltpu.VMEM((local_rows, local_cols), bf16),
            pltpu.VMEM((local_rows, local_cols), bf16),
            pltpu.VMEM((rows, local_cols, width), f32),
            pltpu.VMEM((local_cols, width), bf16),
            pltpu.VMEM((local_cols, width), bf16),
            pltpu.VMEM((local_rows, width), f32),
            pltpu.VMEM((4, local_rows, width), f32),
            pltpu.VMEM((2, local_rows, width), f32),
            pltpu.VMEM((4, 2 * width, width), f32),
            dma((2,)), dma, dma((3, rows)), dma((rows,)), dma((3, rows)), dma((rows,)),
            dma, dma((4,)), dma((2,)), dma((2,)), dma((2, rows)), dma((rows,)), dma((rows,)),
            dma((2,)), dma((rows,)), dma((4,)), dma((4,)), dma((4,)), dma((5,)), dma((2,)),
            dma((2,)), dma,
        ],
        compiler_params=pltpu.CompilerParams(
            collective_id=0, has_side_effects=True, vmem_limit_bytes=VMEM_BYTES),
        cost_estimate=pl.CostEstimate(
            flops=flops, bytes_accessed=4 * local_rows * local_cols, transcendentals=0),
    )(separator_inverse, panel, col_mask, row_mask, pivot_inverse)
    return (off, child)


def solution(mesh):
    in_specs = (P("prow", "pcol"), P("pcol", "prow"), P(), P("prow", "pcol"))
    out_specs = (P("prow", "pcol"), P("prow", "pcol"))
    body = fused if (mesh.shape["prow"], mesh.shape["pcol"]) == (8, 4) else local
    return jax.shard_map(body, mesh=mesh, in_specs=in_specs, out_specs=out_specs, check_vma=False)
```

```python
import functools

import jax
import jax.numpy as jnp
from jax import lax
from jax.experimental import pallas as pl
from jax.experimental.pallas import tpu as pltpu
from jax.sharding import PartitionSpec as P

BS = 768
PIECES = 2
STRIP = 64
TILE_ROWS = 512
TILE_DEPTH = 1024
EARLY = 2560
VMEM_BYTES = 62 * 1024 * 1024
MESH = pl.DeviceIdType.MESH


def product(left, right, dims):
    return lax.dot_general(
        left,
        right,
        (dims, ((), ())),
        precision=lax.Precision.HIGH,
        preferred_element_type=jnp.float32,
    )


def spread(value, root, row_index, col_index, rows, cols):
    held = jnp.where(col_index == root, value, 0)
    done = 0
    bit = cols // 2
    while bit:
        pairs = []
        for r in range(rows):
            start = r * cols // rows
            for c in range(cols):
                if (c ^ start) & ~done == 0:
                    pairs.append((r * cols + c, r * cols + (c ^ bit)))
        held = held + lax.ppermute(held, ("prow", "pcol"), pairs)
        done |= bit
        bit //= 2
    return held


def local(separator_inverse, panel, block_rows, pivot_inverse):
    local_rows, local_cols = separator_inverse.shape
    rows, cols = lax.axis_size("prow"), lax.axis_size("pcol")
    row_index, col_index = lax.axis_index("prow"), lax.axis_index("pcol")
    row_blocks, col_blocks = local_rows // BS, local_cols // BS
    col_keep = lax.dynamic_slice_in_dim(block_rows, col_index * col_blocks, col_blocks)
    row_keep = lax.dynamic_slice_in_dim(block_rows, row_index * row_blocks, row_blocks)
    col_keep = jnp.repeat(col_keep.astype(jnp.float32), BS)
    row_keep = jnp.repeat(row_keep.astype(jnp.float32), BS)
    masked = panel * col_keep[:, None]
    width = panel.shape[1]
    piece = max(width // PIECES, 128)
    pieces = width // piece
    group = rows // cols
    offset = row_index * local_rows - col_index * local_cols
    root = row_index * cols // rows
    lefts, rights = [], []
    for g in range(pieces):
        whole = lax.all_gather(masked[:, g * piece : (g + 1) * piece], "prow", axis=1, tiled=True)
        source = lax.dynamic_slice_in_dim(whole, offset, local_rows, 0)
        lefts.append(spread(source, root, row_index, col_index, rows, cols))
        part = product(whole, separator_inverse, ((0,), (1,)))
        share = lax.psum_scatter(part, "pcol", scatter_dimension=0, tiled=True)
        rights.append(share * row_keep[None, :])
    kept = jnp.stack([v.reshape(group, piece, local_rows) for v in rights], axis=1)
    kept = kept.reshape(group * width, local_rows)
    left = jnp.stack([v.reshape(local_rows, rows, piece) for v in lefts], axis=2)
    left = left.reshape(local_rows, rows * width)
    gram_part = product(left, kept, ((0,), (1,)))
    gram_share = lax.psum_scatter(gram_part, "prow", scatter_dimension=0, tiled=True)
    return (-kept.T, pivot_inverse + gram_share)


def device_kernel(geometry, sep_ref, panel_ref, colmask_ref, rowmask_ref, pivot_ref,
                  off_ref, child_ref, mr_ref, gram_z,
                  s_hi, s_lo, m_buf, m_hi, m_lo, p_buf, near, far, gram_x,
                  load_sem, own_sem, gather_send, gather_recv, second_send, second_recv, late_send, late_recv,
                  p_send, near_recv, far_send, far_recv, root_send, root_recv, root_own, out_sem,
                  rows_sem, x_send, x_recv, z_send, z_recv, pivot_sem, child_sem, stage_sem):
    rows, cols, span = geometry
    local_rows, local_cols = s_hi.shape
    width = m_buf.shape[2]
    r, c = lax.axis_index("prow"), lax.axis_index("pcol")
    z, x = r // 2, lax.rem(r, 2)
    y, core = c // 2, lax.rem(c, 2)
    across = (z * 2 + 1 - x, c)
    above, below = (r + 2, c), (r - 2, c)
    mate = (r, y * 2 + 1 - core)
    other = (r, (1 - y) * 2 + core)
    has_above, has_below = z < span - 1, z > 0
    is_root = c == z
    is_relay = c == lax.rem(z + 2, 4)

    own = pltpu.make_async_copy(panel_ref, m_buf.at[r], own_sem)
    own.start()

    half = local_rows // 2

    def tile(i):
        part = pl.ds(pl.multiple_of(lax.rem(i, 2) * half, half), half)
        return pltpu.make_async_copy(
            sep_ref.at[part, pl.ds(pl.multiple_of((i // 2) * width, width), width)],
            p_buf.at[part], load_sem.at[lax.rem(i, 2)])

    tile(0).start()

    barrier = pltpu.get_barrier_semaphore()
    for peer in (across, mate, other):
        pl.semaphore_signal(barrier, inc=1, device_id=peer, device_id_type=MESH)

    @pl.when(has_above)
    def _():
        pl.semaphore_signal(barrier, inc=1, device_id=above, device_id_type=MESH)

    @pl.when(has_below)
    def _():
        pl.semaphore_signal(barrier, inc=1, device_id=below, device_id_type=MESH)

    pl.semaphore_wait(barrier, 3 + has_above.astype(jnp.int32) + has_below.astype(jnp.int32))

    def line(j):
        inner = jnp.logical_and(z > 0, z < span - 1)
        q = jnp.where(jnp.logical_and(inner, j < 2), 1 - j, j)
        return jnp.where(z < 2, q, span - 1 - q)

    def place(k):
        partner = jnp.logical_or(jnp.logical_and(k >= 2, lax.rem(k, 2) == 0), k == 7)
        j = jnp.where(partner, jnp.where(k == 7, 3, (k - 2) // 2), (k + 1) // 2)
        source_z = line(j)
        return source_z * 2 + jnp.where(partner, 1 - x, x), source_z, partner

    def gather(slot, way, target):
        part = pl.ds(0, EARLY // 2)
        return pltpu.make_async_remote_copy(
            src_ref=m_buf.at[slot, part], dst_ref=m_buf.at[slot, part],
            send_sem=gather_send.at[way, slot], recv_sem=gather_recv.at[slot],
            device_id=target, device_id_type=MESH)

    def gather_second(slot, way, target):
        part = pl.ds(EARLY // 2, EARLY // 2)
        return pltpu.make_async_remote_copy(
            src_ref=m_buf.at[slot, part], dst_ref=m_buf.at[slot, part],
            send_sem=second_send.at[way, slot], recv_sem=second_recv.at[slot],
            device_id=target, device_id_type=MESH)

    def gather_late(slot, way, target):
        part = pl.ds(EARLY, local_cols - EARLY)
        return pltpu.make_async_remote_copy(
            src_ref=m_buf.at[slot, part], dst_ref=m_buf.at[slot, part],
            send_sem=late_send.at[way, slot], recv_sem=late_recv.at[slot],
            device_id=target, device_id_type=MESH)

    def goes_up(source_z):
        return jnp.logical_and(source_z <= z, has_above)

    def goes_down(source_z):
        return jnp.logical_and(source_z >= z, has_below)

    def along(copy, slot, source_z, act):
        @pl.when(goes_up(source_z))
        def _():
            act(copy(slot, 1, above))

        @pl.when(goes_down(source_z))
        def _():
            act(copy(slot, 2, below))

    def first_half(slot, source_z, act):
        along(gather, slot, source_z, act)
        act(gather(slot, 0, across))

    def second_half(slot, source_z, act):
        @pl.when(source_z == z)
        def _():
            act(gather_late(slot, 0, across))

        along(gather_late, slot, source_z, act)
        along(gather_second, slot, source_z, act)
        act(gather_second(slot, 0, across))

    def begin(j):
        source_z = line(j)
        slot = source_z * 2 + x
        gather(slot, 0, across).wait_recv()
        first_half(slot, source_z, lambda copy: copy.start())

    def complete(j):
        source_z = line(j)
        slot = source_z * 2 + x
        gather_late(slot, 0, across).wait_recv()
        gather_second(slot, 0, across).wait_recv()
        second_half(slot, source_z, lambda copy: copy.start())

    inner = jnp.logical_and(has_above, has_below)
    outer = jnp.logical_not(inner)

    def at(now, turn, who, act, j):
        @pl.when(jnp.logical_and(now == turn, who))
        def _():
            act(j)

    def passes_on(source_z):
        return jnp.logical_or(goes_up(source_z), goes_down(source_z))

    def pass_on(j):
        source_z = line(j)
        slot = source_z * 2 + 1 - x

        @pl.when(passes_on(source_z))
        def _():
            gather_late(slot, 0, across).wait_recv()
            along(gather_late, slot, source_z, lambda copy: copy.start())

    def to_mate(slot):
        return pltpu.make_async_remote_copy(
            src_ref=m_buf.at[slot, pl.ds(pl.multiple_of(x * local_rows, local_rows), local_rows)],
            dst_ref=mr_ref.at[slot], send_sem=root_send.at[0, slot], recv_sem=root_recv.at[slot],
            device_id=mate, device_id_type=MESH)

    def to_other(slot):
        return pltpu.make_async_remote_copy(
            src_ref=m_buf.at[slot, pl.ds(pl.multiple_of(x * local_rows, local_rows), local_rows)],
            dst_ref=mr_ref.at[slot], send_sem=root_send.at[1, slot], recv_sem=root_recv.at[slot],
            device_id=other, device_id_type=MESH)

    def relay(slot):
        return pltpu.make_async_remote_copy(
            src_ref=mr_ref.at[slot], dst_ref=mr_ref.at[slot],
            send_sem=root_send.at[0, slot], recv_sem=root_recv.at[slot],
            device_id=mate, device_id_type=MESH)

    def keep_own(slot):
        return pltpu.make_async_copy(
            m_buf.at[slot, pl.ds(pl.multiple_of(x * local_rows, local_rows), local_rows)],
            mr_ref.at[slot], root_own.at[slot])

    def partial(slot):
        i = (slot // 4) * 2 + lax.rem(slot, 2)
        return pltpu.make_async_remote_copy(
            src_ref=p_buf, dst_ref=near.at[i], send_sem=p_send, recv_sem=near_recv.at[i],
            device_id=mate, device_id_type=MESH)

    def chip_sum(slot):
        b = lax.rem(slot, 2)
        return pltpu.make_async_remote_copy(
            src_ref=near.at[(slot // 4) * 2 + b], dst_ref=far.at[b],
            send_sem=far_send.at[b], recv_sem=far_recv.at[b],
            device_id=other, device_id_type=MESH)

    def core_of(slot):
        return lax.rem(slot // 2, 2)

    own.wait()
    first_half(r, z, lambda copy: copy.start())
    second_half(r, z, lambda copy: copy.start())

    tiles = 2 * (local_cols // width)

    def split(i, carry):
        @pl.when(i + 1 < tiles)
        def _():
            tile(i + 1).start()

        tile(i).wait()
        columns = pl.ds(pl.multiple_of((i // 2) * width, width), width)

        def strip(t, inner):
            part = pl.ds(pl.multiple_of(lax.rem(i, 2) * half + t * STRIP, STRIP), STRIP)
            value = p_buf[part, :] * colmask_ref[:, columns] * rowmask_ref[(lax.rem(i, 2) * half + t * STRIP) // BS]
            high = value.astype(jnp.bfloat16)
            s_hi[part, columns] = high
            s_lo[part, columns] = (value - high.astype(jnp.float32)).astype(jnp.bfloat16)
            return inner

        return lax.fori_loop(0, half // STRIP, strip, carry)

    lax.fori_loop(0, tiles, split, 0)

    def relay_at(k):
        slot, _, _ = place(k)

        @pl.when(is_relay)
        def _():
            relay(slot).wait_recv()
            relay(slot).start()

    def step(k, carry):
        slot, source_z, partner = place(k)

        at(k, 1, True, complete, 1)
        at(k, 1, inner, complete, 2)
        at(k, 3, outer, complete, 2)
        at(k, 4, inner, complete, 3)
        at(k, 5, outer, complete, 3)

        @pl.when(partner)
        def _():
            gather(slot, 0, across).wait_recv()
            gather_second(slot, 0, across).wait_recv()

            @pl.when(jnp.logical_not(passes_on(source_z)))
            def _():
                gather_late(slot, 0, across).wait_recv()

        for turn, j in ((1, 0), (3, 1), (5, 2), (5, 3)):
            @pl.when(k == turn)
            def _():
                pass_on(j)

        @pl.when(is_root)
        def _():
            to_other(slot).start()
            to_mate(slot).start()
            keep_own(slot).start()

        @pl.when(k > 0)
        def _():
            before, _, _ = place(k - 1)

            @pl.when(core_of(before) != core)
            def _():
                partial(before).wait_send()

        def cut(t, inner):
            part = pl.ds(pl.multiple_of(t * STRIP, STRIP), STRIP)
            value = m_buf[slot, part, :]
            high = value.astype(jnp.bfloat16)
            m_hi[part, :] = high
            m_lo[part, :] = (value - high.astype(jnp.float32)).astype(jnp.bfloat16)
            return inner

        lax.fori_loop(0, local_cols // STRIP, cut, 0)

        def multiply(t, inner):
            part = pl.ds(pl.multiple_of(t * TILE_ROWS, TILE_ROWS), TILE_ROWS)
            total = None
            for d in range(local_cols // TILE_DEPTH):
                depth = pl.ds(d * TILE_DEPTH, TILE_DEPTH)
                a, b = s_hi[part, depth], s_lo[part, depth]
                u, v = m_hi[depth, :], m_lo[depth, :]
                term = (jnp.dot(a, u, preferred_element_type=jnp.float32)
                        + jnp.dot(a, v, preferred_element_type=jnp.float32)
                        + jnp.dot(b, u, preferred_element_type=jnp.float32))
                total = term if total is None else total + term
            p_buf[part, :] = total
            return inner

        lax.fori_loop(0, local_rows // TILE_ROWS, multiply, 0)

        @pl.when(core_of(slot) != core)
        def _():
            partial(slot).start()

        at(k, 0, True, begin, 1)
        at(k, 0, inner, begin, 2)
        at(k, 2, outer, begin, 2)
        at(k, 3, inner, begin, 3)
        at(k, 4, outer, begin, 3)

        @pl.when(k > 0)
        def _():
            relay_at(k - 1)

        @pl.when(core_of(slot) == core)
        def _():
            partial(slot).wait_recv()
            i = (slot // 4) * 2 + lax.rem(slot, 2)

            def add(t, inner):
                part = pl.ds(pl.multiple_of(t * STRIP, STRIP), STRIP)
                near[i, part, :] += p_buf[part, :]
                return inner

            lax.fori_loop(0, local_rows // STRIP, add, 0)

            @pl.when(slot // 4 != y)
            def _():
                chip_sum(slot).start()

        return carry

    lax.fori_loop(0, rows, step, 0)

    last, _, _ = place(rows - 1)

    @pl.when(core_of(last) != core)
    def _():
        partial(last).wait_send()

    relay_at(rows - 1)

    def own_rows(k):
        slot, _, _ = place(k)
        return pltpu.make_async_copy(
            mr_ref.at[slot], m_buf.at[slot, pl.ds(0, local_rows)], rows_sem.at[slot])

    def drain(k, carry):
        slot, source_z, partner = place(k)

        @pl.when(jnp.logical_not(partner))
        def _():
            first_half(slot, source_z, lambda copy: copy.wait_send())
            second_half(slot, source_z, lambda copy: copy.wait_send())

        @pl.when(partner)
        def _():
            along(gather_late, slot, source_z, lambda copy: copy.wait_send())

        @pl.when(is_root)
        def _():
            to_other(slot).wait_send()
            to_mate(slot).wait_send()
            keep_own(slot).wait()

        @pl.when(is_relay)
        def _():
            relay(slot).wait_send()

        @pl.when(jnp.logical_not(jnp.logical_or(is_root, is_relay)))
        def _():
            relay(slot).wait_recv()

        own_rows(k).start()
        return carry

    lax.fori_loop(0, rows, drain, 0)

    def pivot(b):
        return pltpu.make_async_copy(
            pivot_ref.at[:, pl.ds(b * width, width)],
            m_buf.at[0, pl.ds(local_rows + 2 * width + b * width, width)], pivot_sem.at[b])

    def finish(b):
        return pltpu.make_async_copy(
            near.at[y * 2 + b], off_ref.at[:, pl.ds(b * width, width)], out_sem.at[b])

    for b in range(2):
        pivot(b).start()
        mine = c * 2 + b
        chip_sum(mine).wait_recv()

        def total(t, inner):
            part = pl.ds(pl.multiple_of(t * STRIP, STRIP), STRIP)
            value = near[y * 2 + b, part, :] + far[b, part, :]
            near[y * 2 + b, part, :] = value
            high = value.astype(jnp.bfloat16)
            spot = pl.ds(pl.multiple_of(b * local_rows + t * STRIP, STRIP), STRIP)
            m_hi[spot, :] = high
            m_lo[spot, :] = (value - high.astype(jnp.float32)).astype(jnp.bfloat16)
            return inner

        lax.fori_loop(0, local_rows // STRIP, total, 0)
        finish(b).start()

    columns = pl.ds(0, width)

    def gram(slot):
        pltpu.make_async_copy(
            mr_ref.at[slot], m_buf.at[slot, pl.ds(0, local_rows)], rows_sem.at[slot]).wait()

        def cut(t, inner):
            part = pl.ds(pl.multiple_of(t * STRIP, STRIP), STRIP)
            value = m_buf[slot, part, :]
            high = value.astype(jnp.bfloat16)
            s_hi[part, columns] = high
            s_lo[part, columns] = (value - high.astype(jnp.float32)).astype(jnp.bfloat16)
            return inner

        lax.fori_loop(0, local_rows // STRIP, cut, 0)
        for b in range(2):
            sums = None
            for d in range(local_rows // TILE_ROWS):
                part = pl.ds(d * TILE_ROWS, TILE_ROWS)
                spot = pl.ds(b * local_rows + d * TILE_ROWS, TILE_ROWS)
                u, v = s_hi[part, columns], s_lo[part, columns]
                a, e = m_hi[spot, :], m_lo[spot, :]
                term = crossed(u, a) + crossed(u, e) + crossed(v, a)
                sums = term if sums is None else sums + term
            m_buf[slot, pl.ds(local_rows + b * width, width), :] = sums

    block = pl.ds(local_rows, 2 * width)

    def over_x(slot, source_z):
        return pltpu.make_async_remote_copy(
            src_ref=m_buf.at[slot, block], dst_ref=gram_x.at[source_z],
            send_sem=x_send.at[source_z], recv_sem=x_recv.at[source_z],
            device_id=across, device_id_type=MESH)

    def over_z(slot, source_z, spot, target):
        return pltpu.make_async_remote_copy(
            src_ref=m_buf.at[slot, block], dst_ref=gram_z.at[spot],
            send_sem=z_send.at[source_z], recv_sem=z_recv.at[spot],
            device_id=target, device_id_type=MESH)

    def add_to(slot, ref, spot):
        def one(t, inner):
            part = pl.ds(pl.multiple_of(t * STRIP, STRIP), STRIP)
            here = pl.ds(pl.multiple_of(local_rows + t * STRIP, STRIP), STRIP)
            m_buf[slot, here, :] += ref[spot, part, :]
            return inner

        lax.fori_loop(0, 2 * width // STRIP, one, 0)

    stage = local_rows + 4 * width

    def add_staged(slot, spot):
        copy = pltpu.make_async_copy(
            gram_z.at[spot], m_buf.at[slot, pl.ds(stage, 2 * width)], stage_sem)
        copy.start()
        copy.wait()

        def one(t, inner):
            part = pl.ds(pl.multiple_of(stage + t * STRIP, STRIP), STRIP)
            here = pl.ds(pl.multiple_of(local_rows + t * STRIP, STRIP), STRIP)
            m_buf[slot, here, :] += m_buf[slot, part, :]
            return inner

        lax.fori_loop(0, 2 * width // STRIP, one, 0)

    def send_x(i, carry):
        source_z = line(span - 1 - i)
        slot = source_z * 2 + 1 - x
        gram(slot)
        over_x(slot, source_z).start()
        return carry

    lax.fori_loop(0, span, send_x, 0)

    def down_spot(source_z):
        return jnp.where(source_z == z - 1, span, source_z)

    def send_z(i, carry):
        source_z = line(span - 1 - i)
        slot = source_z * 2 + x
        gram(slot)
        over_x(slot, source_z).wait_recv()
        add_to(slot, gram_x, source_z)

        @pl.when(jnp.logical_and(source_z >= z, has_below))
        def _():
            over_z(slot, source_z, source_z, above).wait_recv()
            add_staged(slot, source_z)

        @pl.when(jnp.logical_and(source_z <= z, has_above))
        def _():
            spot = jnp.where(source_z == z, span, source_z)
            over_z(slot, source_z, spot, below).wait_recv()
            add_staged(slot, spot)

        @pl.when(source_z > z)
        def _():
            over_z(slot, source_z, source_z, above).start()

        @pl.when(source_z < z)
        def _():
            over_z(slot, source_z, down_spot(source_z), below).start()

        return carry

    lax.fori_loop(0, span, send_z, 0)

    def child(b):
        return pltpu.make_async_copy(
            p_buf.at[pl.ds(b * width, width)], child_ref.at[:, pl.ds(b * width, width)],
            child_sem.at[b])

    for b in range(2):
        pivot(b).wait()

        def subtract(t, inner):
            part = pl.ds(pl.multiple_of(b * width + t * STRIP, STRIP), STRIP)
            here = pl.ds(pl.multiple_of(local_rows + b * width + t * STRIP, STRIP), STRIP)
            base = pl.ds(pl.multiple_of(local_rows + (2 + b) * width + t * STRIP, STRIP), STRIP)
            p_buf[part, :] = m_buf[0, base, :] - m_buf[r, here, :]
            return inner

        lax.fori_loop(0, width // STRIP, subtract, 0)
        child(b).start()

    def settle(i, carry):
        over_x(i * 2 + 1 - x, i).wait_send()

        @pl.when(i > z)
        def _():
            over_z(i * 2 + x, i, i, above).wait_send()

        @pl.when(i < z)
        def _():
            over_z(i * 2 + x, i, down_spot(i), below).wait_send()

        return carry

    lax.fori_loop(0, span, settle, 0)
    for b in range(2):
        chip_sum((1 - y) * 4 + core * 2 + b).wait_send()
        finish(b).wait()
        child(b).wait()


def crossed(left, right):
    return lax.dot_general(
        left, right, (((0,), (0,)), ((), ())), preferred_element_type=jnp.float32)


def fused(separator_inverse, panel, block_rows, pivot_inverse):
    local_rows, local_cols = separator_inverse.shape
    width = panel.shape[1]
    rows, cols = lax.axis_size("prow"), lax.axis_size("pcol")
    row_index, col_index = lax.axis_index("prow"), lax.axis_index("pcol")
    row_blocks, col_blocks = local_rows // BS, local_cols // BS
    col_keep = lax.dynamic_slice_in_dim(block_rows, col_index * col_blocks, col_blocks)
    row_keep = lax.dynamic_slice_in_dim(block_rows, row_index * row_blocks, row_blocks)
    col_mask = jnp.repeat(col_keep.astype(jnp.float32), BS)[None, :]
    row_mask = -jnp.broadcast_to(
        row_keep.astype(jnp.float32)[:, None, None], (row_blocks, 1, width))
    dma, f32, bf16 = pltpu.SemaphoreType.DMA, jnp.float32, jnp.bfloat16
    flops = 6 * local_rows * local_cols * rows * width
    off, child, _, _ = pl.pallas_call(
        functools.partial(device_kernel, (rows, cols, rows // 2)),
        out_shape=(jax.ShapeDtypeStruct((local_rows, 2 * width), f32),
                   jax.ShapeDtypeStruct((width, 2 * width), f32),
                   jax.ShapeDtypeStruct((rows, local_rows, width), f32),
                   jax.ShapeDtypeStruct((5, 2 * width, width), f32)),
        in_specs=[pl.BlockSpec(memory_space=pl.ANY), pl.BlockSpec(memory_space=pl.ANY),
                  pl.BlockSpec(memory_space=pltpu.VMEM), pl.BlockSpec(memory_space=pltpu.VMEM),
                  pl.BlockSpec(memory_space=pl.ANY)],
        out_specs=(pl.BlockSpec(memory_space=pl.ANY),) * 4,
        scratch_shapes=[
            pltpu.VMEM((local_rows, local_cols), bf16),
            pltpu.VMEM((local_rows, local_cols), bf16),
            pltpu.VMEM((rows, local_cols, width), f32),
            pltpu.VMEM((local_cols, width), bf16),
            pltpu.VMEM((local_cols, width), bf16),
            pltpu.VMEM((local_rows, width), f32),
            pltpu.VMEM((4, local_rows, width), f32),
            pltpu.VMEM((2, local_rows, width), f32),
            pltpu.VMEM((4, 2 * width, width), f32),
            dma((2,)), dma, dma((3, rows)), dma((rows,)), dma((3, rows)), dma((rows,)),
            dma((3, rows)), dma((rows,)),
            dma, dma((4,)), dma((2,)), dma((2,)), dma((2, rows)), dma((rows,)), dma((rows,)),
            dma((2,)), dma((rows,)), dma((4,)), dma((4,)), dma((4,)), dma((5,)), dma((2,)),
            dma((2,)), dma,
        ],
        compiler_params=pltpu.CompilerParams(
            collective_id=0, has_side_effects=True, vmem_limit_bytes=VMEM_BYTES),
        cost_estimate=pl.CostEstimate(
            flops=flops, bytes_accessed=4 * local_rows * local_cols, transcendentals=0),
    )(separator_inverse, panel, col_mask, row_mask, pivot_inverse)
    return (off, child)


def solution(mesh):
    in_specs = (P("prow", "pcol"), P("pcol", "prow"), P(), P("prow", "pcol"))
    out_specs = (P("prow", "pcol"), P("prow", "pcol"))
    body = fused if (mesh.shape["prow"], mesh.shape["pcol"]) == (8, 4) else local
    return jax.shard_map(body, mesh=mesh, in_specs=in_specs, out_specs=out_specs, check_vma=False)
```
